128 devices in a mesh: worker: 8 (over x_lo, z), shard: 16 (over y, x_hi, core).
Axes of the slice: x: 4 (x_hi: 2, x_lo: 2; x = x_hi * 2 + x_lo), y: 4, z: 4, core: 2. Of those that a mesh axis runs over, the one named last changes fastest.
Arguments:
- token_ids: int32 [32768], P(('worker', 'shard')), may hold values from 0 to 16383, as said below
- cotangent: bfloat16 [32768, 1024], P(('worker', 'shard')), may hold values from -6 to 6
- embedding: bfloat16 [16384, 7168], P(('worker', 'shard')), may hold values from -6 to 6
- weight: bfloat16 [8, 7168, 1024], P('worker', 'shard'), may hold values from -6 to 6
- anchor: float32 [7168, 256], P('shard', 'worker'), may hold values from -6 to 6
- momentum: float32 [7168, 256], P('shard', 'worker'), may hold values from -3 to 3
- due_fragment: int32 [1], replicated, may hold values from 0 to 4095
Outputs:
- new_weight: bfloat16 [8, 7168, 1024], P('worker', 'shard')
- new_anchor: float32 [7168, 256], P('shard', 'worker')
- new_momentum: float32 [7168, 256], P('shard', 'worker')
The draws below stay inside these ranges and needn't reach their ends.
Inputs may be any that keep to these rules, and one draw needn't show every extreme that they name: `token_ids`: among the 256 tokens of one device, at most 2 ids fall in any one device's block of 128 embedding rows, and exactly 2 fall in some block.
All inputs are finite; a program needn't handle non-finite values.
Results may differ from the reference program's by a relative error of at most 0.012.
Values may be sent and summed in bfloat16 or wider, within the bound.
A program may use at most 128 MiB of HBM per device.

```python
import jax
import jax.numpy as jnp
from jax import lax

D = 7168
KVW = 1024
VOC = 16384
FRAGS = 4
TOK_DEV = 256
REPLICAS = 8
OWNERS = 128
TOK_REP = 4096
TOKENS = 32768
RPD = 128
CAP = 2
FC = 256


def draw_token_ids(key, part):
    key = jax.random.fold_in(key, 11)

    def one_block(block_key):
        key_crowd, key_pool, key_order, key_offset = jax.random.split(block_key, 4)
        crowded = jax.random.randint(key_crowd, (), 0, OWNERS)
        others_pool = jax.random.permutation(key_pool, (OWNERS - 1) * CAP) // CAP
        others = others_pool[:TOK_DEV - CAP]
        others = others + (others >= crowded).astype(jnp.int32)
        owner_list = jnp.concatenate([jnp.full((CAP,), crowded, jnp.int32), others.astype(jnp.int32)])
        owner_list = jax.random.permutation(key_order, owner_list)
        offsets = jax.random.randint(key_offset, (TOK_DEV,), 0, RPD)
        return owner_list * RPD + offsets
    blocks = jax.vmap(one_block)(jax.random.split(key, OWNERS))
    return blocks.reshape(TOKENS).astype(jnp.int32)


def block_scale(own_key, extent, shards, low, top_value):
    factor_of, own = 1.0, jax.random.fold_in(own_key, 6)
    for axis_at, shards_of in shards:
        heights = jnp.exp(jax.random.uniform(jax.random.fold_in(own, axis_at), (shards_of,), jnp.float32, low / len(shards), top_value / len(shards)))
        factor_of = factor_of * jnp.repeat(heights, extent[axis_at] // shards_of).reshape([-1 if axis == axis_at else 1 for axis in range(len(extent))])
    return factor_of


def noise(key, dims, scale, reach, cuts=(), kind=jnp.bfloat16):
    drawn = jax.random.normal(key, dims, jnp.float32) * scale
    if len(cuts) > 0:
        drawn = block_scale(key, dims, cuts, -0.22, 0.18) * drawn
    return jnp.clip(drawn, min=-reach, max=reach).astype(kind)


def setup_inputs(seed: int = 0) -> dict:
    streams_of = jax.random.split(jax.random.key(seed), 8)
    return {
        "token_ids": draw_token_ids(jax.random.fold_in(streams_of[7], 71), 0),
        "cotangent": noise(streams_of[1], (TOKENS, KVW), 1.0, 6.0, ((0, 128),)),
        "embedding": noise(streams_of[2], (VOC, D), 1.0, 6.0, ((0, 128),)),
        "weight": noise(streams_of[3], (REPLICAS, D, KVW), 1.0, 6.0, ((0, 8), (1, 16))),
        "anchor": noise(streams_of[4], (D, FC), 1.0, 6.0, ((0, 16), (1, 8)), jnp.float32),
        "momentum": noise(streams_of[5], (D, FC), 0.5, 3.0, ((0, 16), (1, 8)), jnp.float32),
        "due_fragment": jax.random.randint(streams_of[6], (1,), 0, 1024 * FRAGS).astype(jnp.int32),
    }


epsilon = 1e-06
inner_rate = 1.0
outer_rate = 0.7
outer_decay = 0.9
mix_share = 0.5

def reference(token_ids, cotangent, embedding, weight, anchor, momentum, due_fragment):
    weight_scale = D ** (-0.5)
    col_start = (due_fragment[0] % FRAGS * FC).astype(jnp.int32)
    blocks_per = TOK_REP // TOK_DEV
    stepped_all = []
    frag_total = jnp.zeros((D, FC), jnp.float32)
    for replica in range(REPLICAS):
        ids_rep = token_ids[replica * TOK_REP:(replica + 1) * TOK_REP]
        embedded = embedding[ids_rep].astype(jnp.float32)
        rows_n = (embedded * lax.rsqrt(lax.optimization_barrier(jnp.mean(embedded * embedded, axis=1, keepdims=True)) + epsilon)).astype(jnp.bfloat16)
        rows_c = cotangent[replica * TOK_REP:(replica + 1) * TOK_REP].astype(jnp.float32)
        weight_rep = weight[replica]
        preact = jnp.dot(rows_n, weight_rep, preferred_element_type=jnp.float32) * weight_scale
        sig_val = jax.nn.sigmoid(preact)
        grad_pre = (rows_c * sig_val * (1.0 + preact * (1.0 - sig_val))).astype(jnp.bfloat16)
        grads = jnp.zeros((D, KVW), jnp.float32)
        for block in range(blocks_per):
            part_n = rows_n[block * TOK_DEV:(block + 1) * TOK_DEV]
            part_g = grad_pre[block * TOK_DEV:(block + 1) * TOK_DEV]
            product = jnp.dot(part_n.T, part_g, preferred_element_type=jnp.float32) * weight_scale
            product = lax.optimization_barrier(product.astype(jnp.bfloat16))
            grads = grads + product.astype(jnp.float32)
        weight_f = weight_rep.astype(jnp.float32)
        stepped_all.append(weight_f - inner_rate * grads)
        frag_total = frag_total + lax.dynamic_slice_in_dim(weight_f, col_start, FC, 1)
    replica_mean = frag_total / REPLICAS
    delta = anchor - replica_mean
    new_momentum = outer_decay * momentum + delta
    new_anchor = anchor - outer_rate * (delta + outer_decay * new_momentum)
    outputs = []
    for replica in range(REPLICAS):
        stepped = stepped_all[replica]
        mixed = mix_share * lax.dynamic_slice_in_dim(stepped, col_start, FC, 1) + (1.0 - mix_share) * new_anchor
        outputs.append(lax.dynamic_update_slice_in_dim(stepped, mixed, col_start, 1).astype(jnp.bfloat16))
    new_weight = jnp.stack(outputs, axis=0)
    return (new_weight, new_anchor, new_momentum)
```

```python
import functools

import jax
import jax.numpy as jnp
from jax import lax
from jax.experimental import pallas as pl
from jax.experimental.pallas import tpu as pltpu
from jax.sharding import PartitionSpec as P

epsilon = 1e-06
inner_rate = 1.0
outer_rate = 0.7
outer_decay = 0.9
mix_share = 0.5

MESH = pl.DeviceIdType.MESH
f32, bf16, i32 = jnp.float32, jnp.bfloat16, jnp.int32


def iota(shape, dim):
    return lax.broadcasted_iota(i32, shape, dim)


def onehot(cond):
    return jnp.where(cond, 1.0, 0.0).astype(bf16)


def dot(a, b, ca=1, cb=0):
    return lax.dot_general(a, b, (((ca,), (cb,)), ((), ())), preferred_element_type=f32)


def m4(v):
    return lax.rem(v + 8, 4)


def kernel(
    ids_ref, fcol_ref, anchor_ref, mom_ref, emb_hbm, weight_hbm, cot_hbm,
    out_ref, new_anchor_ref, new_mom_ref,
    emb, normed, cot, ids_g, ids_all, SS, RA, RB, N, NT, WF,
    cot_send, cot_recv, cot_rows, fpad, f_send, f_recv, a_send, a_recv, full_anchor,
    acc, px_send, px_recv, G, PB, own_acc, CS, CR, S2, SL, SR, R2, RL, RR, nap,
    lsem, ssem, rsem,
):
    w = lax.axis_index("worker")
    s = lax.axis_index("shard")
    x_lo, z = w // 4, lax.rem(w, 4)
    y, x_hi, c = s // 4, lax.rem(s // 2, 2), lax.rem(s, 2)
    x = x_hi * 2 + x_lo
    width = emb.shape[1]
    half = width // 2
    chunk = width // 8
    scale = width ** (-0.5)
    rows = WF.shape[2]
    hr = rows // 2

    def dev(xx, yy, zz, cc):
        return (lax.rem(xx, 2) * 4 + zz, yy * 4 + (xx // 2) * 2 + cc)

    counter = [0]

    def send(src, dst, to):
        i = counter[0]
        counter[0] += 1
        copy = pltpu.make_async_remote_copy(
            src_ref=src, dst_ref=dst, send_sem=ssem.at[i], recv_sem=rsem.at[i],
            device_id=to, device_id_type=MESH,
        )
        copy.start()
        started.append(copy)
        return copy

    started = []

    zs = [dev(x, y, m4(z + d), c) for d in (1, 2, 3)]
    xs = [dev(m4(x + d), y, z, c) for d in (1, 2, 3)]
    x_flip = x_hi * 2 + 1 - x_lo
    workers = [(d, e) for d in (0, 1) for e in range(4) if (d, e) != (0, 0)]
    worker_of = lambda d, e: lax.rem(x_lo + d, 2) * 4 + m4(z + e)
    shards = [(d, h, k) for d in range(4) for h in (0, 1) for k in (0, 1) if (d, h, k) != (0, 0, 0)]
    shard_of = lambda d, h, k: m4(y + d) * 4 + lax.rem(x_hi + h, 2) * 2 + lax.rem(c + k, 2)

    emb_copy = pltpu.make_async_copy(emb_hbm, emb, lsem.at[0])
    weight_copy = pltpu.make_async_copy(weight_hbm, WF.at[y, c], lsem.at[1])
    cot_copy = pltpu.make_async_copy(cot_hbm, cot, lsem.at[2])
    emb_copy.start()
    weight_copy.start()
    cot_copy.start()

    barrier = pltpu.get_barrier_semaphore()
    n_partners = 0
    for d, e in workers:
        pl.semaphore_signal(barrier, inc=1, device_id=(worker_of(d, e), s), device_id_type=MESH)
        n_partners += 1
    for o in shards:
        pl.semaphore_signal(barrier, inc=1, device_id=(w, shard_of(*o)), device_id_type=MESH)
        n_partners += 1
    for d in (1, 3):
        pass
    pl.semaphore_signal(barrier, inc=1, device_id=dev(m4(x_flip + 2), y, z, c), device_id_type=MESH)
    n_partners += 1
    pl.semaphore_wait(barrier, n_partners)

    ids = ids_ref[...]
    ids_g[w] = jnp.broadcast_to(ids, (8, 256))
    first = [send(ids_g.at[w], ids_g.at[w], (worker_of(d, e), s)) for d, e in workers]

    emb_copy.wait()
    n_rows = emb.shape[0]
    total = jnp.zeros((n_rows, 128), f32)

    def add_square(t, total):
        v = emb[:, pl.ds(pl.multiple_of(t * 128, 128), 128)].astype(f32)
        return total + v * v

    total = lax.fori_loop(0, width // 128, add_square, total)
    factor = lax.rsqrt(jnp.sum(total, axis=1, keepdims=True) / width + epsilon)

    def scale_rows(t, carry):
        at = pl.ds(pl.multiple_of(t * 128, 128), 128)
        normed[:, at] = (emb[:, at].astype(f32) * factor).astype(bf16)
        return carry

    lax.fori_loop(0, width // 128, scale_rows, 0)

    for copy in first:
        copy.wait_recv()
    row8 = iota((8, 256), 0)
    tile = ids_g[0]
    for i in range(1, 8):
        tile = jnp.where(row8 == i, ids_g[i], tile)
    ids_all[s] = tile
    second = [send(ids_all.at[s], ids_all.at[s], (w, shard_of(*o))) for o in shards]

    sib = (w, s + 1 - 2 * c)
    up, down = (w, m4(y + 1) * 4 + lax.rem(s, 4)), (w, m4(y + 3) * 4 + lax.rem(s, 4))
    weight_copy.wait()
    for copy in second:
        copy.wait_recv()
    w_up = send(WF.at[y, c], WF.at[y, c], up)
    w_down = send(WF.at[y, c], WF.at[y, c], down)
    w_sib = [send(WF.at[y, c], WF.at[y, c], sib)]

    me = w * 16 + s
    asked = ids_all[...].reshape(128, 256)
    local = lax.rem(asked, 128).astype(f32)
    mine = (asked // 128) == me
    low = jnp.min(jnp.where(mine, local, 999.0), axis=1, keepdims=True)
    high = jnp.max(jnp.where(mine, local, -1.0), axis=1, keepdims=True)
    r_out, r_in = iota((128, 128), 0), iota((128, 128), 1)
    turn = onehot(r_in == lax.rem(r_out, 16) * 8 + r_out // 16)
    lane = iota((128, 128), 1).astype(f32)
    for k, pick in ((0, low), (1, high)):
        sel = dot(turn, onehot(lane == pick)).astype(bf16)
        for q in range(8):
            got = dot(sel, normed[:, q * chunk:(q + 1) * chunk]).astype(bf16)
            yq, h = q // 2, q % 2
            for ww in range(8):
                xd, zd = h * 2 + ww // 4, ww % 4
                a, b = (zd, xd) if k == 0 else (xd, zd)
                SS[k, a, b, :, yq * chunk:(yq + 1) * chunk] = got[ww * 16:(ww + 1) * 16]

    A, B, direct = [], [], []
    for d in (1, 3, 2):
        A.append((d, send(SS.at[0, m4(z + d)], RA.at[z], dev(x, y, m4(z + d), c))))
        B.append((d, send(SS.at[1, m4(x + d)], RB.at[x], dev(m4(x + d), y, z, c))))
    arrive = []
    for d in (1, 3, 2):
        arrive.append(send(SS.at[0, z, m4(x + d)], N.at[x, z, 0], dev(m4(x + d), y, z, c)))
        arrive.append(send(SS.at[1, x, m4(z + d)], N.at[x, z, 1], dev(x, y, m4(z + d), c)))
    N[x, z, 0] = SS[0, z, x]
    N[x, z, 1] = SS[1, x, z]

    cot_copy.wait()
    er, ec = iota((256, 256), 0), iota((256, 256), 1)
    idf = ids.astype(f32)
    id_row = jnp.broadcast_to(idf, (256, 256))
    id_col = jnp.sum(jnp.where(er == ec, id_row, 0.0), axis=1, keepdims=True)
    own_row = jnp.broadcast_to((ids // 128).astype(f32), (256, 256))
    own_col = jnp.sum(jnp.where(er == ec, own_row, 0.0), axis=1, keepdims=True)
    before = (own_col == own_row) & ((id_col < id_row) | ((id_col == id_row) & (er < ec)))
    rank = jnp.sum(jnp.where(before, 1.0, 0.0), axis=0, keepdims=True).astype(i32)
    owner = ids // 128
    place = lax.rem(owner, 16) * 16 + (owner // 16) * 2 + rank
    cot_send[...] = dot(onehot(er == place), cot[...]).astype(bf16).reshape(cot_send.shape)
    cots = [send(cot_send.at[shard_of(*o)], cot_recv.at[s], (w, shard_of(*o))) for o in shards]
    cot_recv[s] = cot_send[s]

    fcol = fcol_ref[...]
    due = [jnp.where(fcol == j, 1.0, 0.0) for j in range(4)]
    own_w = WF.at[y, c]
    frag = own_w[:, 0:256].astype(f32) * due[0]
    for j in range(1, 4):
        frag += own_w[:, j * 256:(j + 1) * 256].astype(f32) * due[j]
    fpad[rows:] = jnp.zeros((fpad.shape[0] - rows, 256), bf16)
    fpad[:rows] = frag.astype(bf16)
    eye = onehot(er == ec)
    f_send[...] = dot(eye, fpad[...], 1, 1).astype(bf16).reshape(f_send.shape)
    frags = [send(f_send.at[worker_of(d, e)], f_recv.at[w], (worker_of(d, e), s)) for d, e in workers]
    f_recv[w] = f_send[w]

    for (d, a), (_, b) in zip(A, B):
        a.wait_recv()
        zf = m4(z - d)
        for e in (1, 3, 2):
            arrive.append(send(RA.at[zf, m4(x + e)], N.at[x, zf, 0], dev(m4(x + e), y, z, c)))
        N[x, zf, 0] = RA[zf, x]
        b.wait_recv()
        xf = m4(x - d)
        for e in (1, 3, 2):
            arrive.append(send(RB.at[xf, m4(z + e)], N.at[xf, z, 1], dev(x, y, m4(z + e), c)))
        N[xf, z, 1] = RB[xf, z]

    yu, yd = m4(y + 1), m4(y + 3)
    y2 = m4(y + 2)
    w_up.wait_recv()
    w_far_up = send(WF.at[yd, c, 0:hr], WF.at[yd, c, 0:hr], up)
    w_sib.append(send(WF.at[yd, c], WF.at[yd, c], sib))
    w_down.wait_recv()
    w_far_down = send(WF.at[yu, c, hr:rows], WF.at[yu, c, hr:rows], down)
    w_sib.append(send(WF.at[yu, c], WF.at[yu, c], sib))
    w_far_up.wait_recv()
    w_sib.append(send(WF.at[y2, c, 0:hr], WF.at[y2, c, 0:hr], sib))
    w_far_down.wait_recv()
    w_sib.append(send(WF.at[y2, c, hr:rows], WF.at[y2, c, hr:rows], sib))

    for copy in frags:
        copy.wait_recv()
    sel32 = onehot(lax.rem(iota((256, 32), 0), 32) == iota((256, 32), 1))
    mean = dot(f_recv[...].reshape(256, 512), sel32, 0, 0)[:rows] / 8
    anchor = anchor_ref[...]
    delta = anchor - mean
    new_mom = outer_decay * mom_ref[...] + delta
    new_anchor = anchor - outer_rate * (delta + outer_decay * new_mom)
    new_mom_ref[...] = new_mom
    new_anchor_ref[...] = new_anchor
    nap[...] = jnp.zeros_like(nap)
    nap[:rows] = new_anchor.astype(bf16)
    eye32 = onehot(iota((32, 32), 0) == iota((32, 32), 1))
    a_send[...] = dot(eye32, nap[...], 1, 1).astype(bf16)
    anchors = [send(a_send, a_recv.at[w], (worker_of(d, e), s)) for d, e in workers]
    a_recv[w] = a_send[...]

    for copy in cots:
        copy.wait_recv()
    back = onehot(ec == lax.rem(er, 16) * 16 + er // 16)
    cot_rows[...] = dot(back, cot_recv[...].reshape(256, 1024)).astype(bf16)

    for copy in w_sib:
        copy.wait_recv()
    for copy in arrive:
        copy.wait_recv()

    cols = lambda j: slice(j * 256, (j + 1) * 256)
    x_pair = (w, y * 4 + (1 - x_hi) * 2 + c)
    px, gx, core, far, near = {}, {}, {}, {}, {}

    def forward(j):
        part = None
        for kk in range(4):
            a = N[:, :, :, :, kk * chunk:(kk + 1) * chunk].reshape(512, chunk)
            b = WF[kk].reshape(chunk, WF.shape[3])[:, cols(j)]
            p = dot(a, b)
            part = p if part is None else part + p
        acc[j % 2] = (part * scale).reshape(2, 256, 256)
        px_send[j] = acc[j % 2, 1 - x_hi].astype(bf16)
        px[j] = send(px_send.at[j], px_recv.at[j], x_pair)

    def pointwise(j):
        px[j].wait_recv()
        pre = acc[j % 2, x_hi] + px_recv[j].astype(f32)
        sig = jax.nn.sigmoid(pre)
        g = cot_rows[:, cols(j)].astype(f32) * sig * (1.0 + pre * (1.0 - sig))
        G[j, x_hi] = g.astype(bf16)
        gx[j] = send(G.at[j, x_hi], G.at[j, x_hi], x_pair)

    def turned():
        for q in range(half // 256):
            part = N[:, :, :, :, q * 256:(q + 1) * 256].reshape(512, 256)
            NT[q * 256:(q + 1) * 256] = dot(eye, part, 1, 1).astype(bf16)

    order = (2, 1, 3, 0)

    def backward(j):
        gx[j].wait_recv()
        g = G[j].reshape(512, 256)
        for d in order:
            yy = m4(y + d)
            base = yy * chunk
            other = NT[pl.ds(pl.multiple_of(base + (1 - c) * rows, 16), rows)]
            CS[j, d] = (dot(other, g) * scale).astype(bf16)
            core[j, d] = send(CS.at[j, d], CR.at[j, d], sib)
            own = NT[pl.ds(pl.multiple_of(base + c * rows, 16), rows)]
            PB[d] = dot(own, g) * scale

    def join(j):
        for d in order:
            core[j, d].wait_recv()
            t = PB[d] + CR[j, d].astype(f32)
            if d == 2:
                S2[j] = t.astype(bf16)
                far[j] = (
                    send(S2.at[j, 0:hr], R2.at[j, 0], up),
                    send(S2.at[j, hr:rows], R2.at[j, 1], down),
                )
            elif d == 1:
                SL[j, hr:rows] = t[hr:rows].astype(bf16)
                near[j] = [send(SL.at[j, hr:rows], RL.at[j, hr:rows], up)]
                PB[1, 0:hr] = t[0:hr]
            elif d == 3:
                SR[j, 0:hr] = t[0:hr].astype(bf16)
                near[j].append(send(SR.at[j, 0:hr], RR.at[j, 0:hr], down))
                PB[3, hr:rows] = t[hr:rows]
            else:
                own_acc[j] = t

    def pass_on(j):
        far[j][0].wait_recv()
        SL[j, 0:hr] = (PB[1, 0:hr] + R2[j, 0].astype(f32)).astype(bf16)
        near[j].append(send(SL.at[j, 0:hr], RL.at[j, 0:hr], up))
        far[j][1].wait_recv()
        SR[j, hr:rows] = (PB[3, hr:rows] + R2[j, 1].astype(f32)).astype(bf16)
        near[j].append(send(SR.at[j, hr:rows], RR.at[j, hr:rows], down))

    def finish(j):
        for copy in near[j]:
            copy.wait_recv()
        grads = own_acc[j] + RL[j].astype(f32) + RR[j].astype(f32)
        stepped = own_w[:, cols(j)].astype(f32) - inner_rate * grads
        share = due[j] * (1.0 - mix_share)
        out_ref[:, cols(j)] = (stepped * (1.0 - share) + share * full_anchor[...]).astype(bf16)

    forward(0)
    forward(1)
    turned()
    for copy in anchors:
        copy.wait_recv()
    full_anchor[...] = dot(a_recv[...].reshape(256, 512), eye, 0, 0)[:rows]
    pointwise(0)
    forward(2)
    pointwise(1)
    backward(0)
    join(0)
    pass_on(0)
    forward(3)
    pointwise(2)
    backward(1)
    join(1)
    pass_on(1)
    pointwise(3)
    backward(2)
    join(2)
    finish(0)
    pass_on(2)
    backward(3)
    join(3)
    finish(1)
    pass_on(3)
    finish(2)
    finish(3)

    for copy in started:
        copy.wait_send()


def shards(token_ids, cotangent, embedding, weight, anchor, momentum, due_fragment):
    rows, width = weight.shape[1], embedding.shape[1]
    half = width // 2
    fcol = jnp.full((1, 256), due_fragment[0] % 4, i32)
    vmem = pl.BlockSpec(memory_space=pltpu.VMEM)
    anyspace = pl.BlockSpec(memory_space=pl.ANY)
    V = pltpu.VMEM
    n_sends = 160
    new_weight, new_anchor, new_momentum = pl.pallas_call(
        kernel,
        out_shape=(
            jax.ShapeDtypeStruct((rows, 1024), bf16),
            jax.ShapeDtypeStruct(anchor.shape, f32),
            jax.ShapeDtypeStruct(anchor.shape, f32),
        ),
        in_specs=[vmem] * 4 + [anyspace] * 3,
        out_specs=(vmem, vmem, vmem),
        scratch_shapes=[
            V((128, width), bf16),
            V((128, width), bf16),
            V((256, 1024), bf16),
            V((8, 8, 256), i32),
            V((16, 8, 256), i32),
            V((2, 4, 4, 16, half), bf16),
            V((4, 4, 16, half), bf16),
            V((4, 4, 16, half), bf16),
            V((4, 4, 2, 16, half), bf16),
            V((half, 512), bf16),
            V((4, 2, rows, 1024), bf16),
            V((16, 16, 1024), bf16),
            V((16, 16, 1024), bf16),
            V((256, 1024), bf16),
            V((512, 256), bf16),
            V((8, 32, 512), bf16),
            V((8, 32, 512), bf16),
            V((32, 512), bf16),
            V((8, 32, 512), bf16),
            V((rows, 256), f32),
            V((2, 2, 256, 256), f32),
            V((4, 256, 256), bf16),
            V((4, 256, 256), bf16),
            V((4, 2, 256, 256), bf16),
            V((4, rows, 256), f32),
            V((4, rows, 256), f32),
            V((4, 4, rows, 256), bf16),
            V((4, 4, rows, 256), bf16),
            V((4, rows, 256), bf16),
            V((4, rows, 256), bf16),
            V((4, rows, 256), bf16),
            V((4, 2, rows // 2, 256), bf16),
            V((4, rows, 256), bf16),
            V((4, rows, 256), bf16),
            V((512, 32), bf16),
            pltpu.SemaphoreType.DMA((4,)),
            pltpu.SemaphoreType.DMA((n_sends,)),
            pltpu.SemaphoreType.DMA((n_sends,)),
        ],
        compiler_params=pltpu.CompilerParams(
            collective_id=0, has_side_effects=True, vmem_limit_bytes=60 * 2**20
        ),
        cost_estimate=pl.CostEstimate(flops=7_500_000_000, bytes_accessed=5_000_000, transcendentals=262144),
        name="diloco_step",
    )(token_ids.reshape(1, 256), fcol, anchor, momentum, embedding, weight.reshape(rows, 1024), cotangent)
    return (new_weight[None], new_anchor, new_momentum)


def solution(mesh):
    placed = (
        P(("worker", "shard")),
        P(("worker", "shard"), None),
        P(("worker", "shard"), None),
        P("worker", "shard", None),
        P("shard", "worker"),
        P("shard", "worker"),
        P(),
    )
    return jax.shard_map(
        shards,
        mesh=mesh,
        in_specs=placed,
        out_specs=(P("worker", "shard", None), P("shard", "worker"), P("shard", "worker")),
        check_vma=False,
    )
```

```python
import functools

import jax
import jax.numpy as jnp
from jax import lax
from jax.experimental import pallas as pl
from jax.experimental.pallas import tpu as pltpu
from jax.sharding import PartitionSpec as P

epsilon = 1e-06
inner_rate = 1.0
outer_rate = 0.7
outer_decay = 0.9
mix_share = 0.5

MESH = pl.DeviceIdType.MESH
f32, bf16, i32 = jnp.float32, jnp.bfloat16, jnp.int32


def iota(shape, dim):
    return lax.broadcasted_iota(i32, shape, dim)


def onehot(cond):
    return jnp.where(cond, 1.0, 0.0).astype(bf16)


def dot(a, b, ca=1, cb=0):
    return lax.dot_general(a, b, (((ca,), (cb,)), ((), ())), preferred_element_type=f32)


def m4(v):
    return lax.rem(v + 8, 4)


def kernel(
    names, sizes,
    ids_ref, due_ref, anchor_ref, mom_ref, emb_hbm, weight_hbm, cot_hbm,
    out_hbm, new_anchor_ref, new_mom_ref, *scratch,
):
    R = dict(zip(names, scratch))
    emb, normed, cot, ids_g, ids_all = (R[n] for n in ("emb", "normed", "cot", "ids_g", "ids_all"))
    SS, RA, RB, N, NT, WF = (R[n] for n in ("SS", "RA", "RB", "N", "NT", "WF"))
    cot_send, cot_far, cot_recv, cot_rows = (R[n] for n in ("cot_send", "cot_far", "cot_recv", "cot_rows"))
    fpad, f_send, f_recv = (R[n] for n in ("fpad", "f_send", "f_recv"))
    a_send, a_recv, full_anchor = (R[n] for n in ("a_send", "a_recv", "full_anchor"))
    PB = R["PB"]
    lsem, ssem, rsem = R["lsem"], R["ssem"], R["rsem"]
    n_cols = len(sizes)
    starts = [sum(sizes[:j]) for j in range(n_cols)]
    w = lax.axis_index("worker")
    s = lax.axis_index("shard")
    x_lo, z = w // 4, lax.rem(w, 4)
    y, x_hi, c = s // 4, lax.rem(s // 2, 2), lax.rem(s, 2)
    x = x_hi * 2 + x_lo
    width = emb.shape[1]
    half = width // 2
    chunk = width // 8
    scale = width ** (-0.5)
    rows = WF.shape[2]
    hr = rows // 2

    def dev(xx, yy, zz, cc):
        return (lax.rem(xx, 2) * 4 + zz, yy * 4 + (xx // 2) * 2 + cc)

    counter = [0]

    def send(src, dst, to):
        i = counter[0]
        counter[0] += 1
        copy = pltpu.make_async_remote_copy(
            src_ref=src, dst_ref=dst, send_sem=ssem.at[i], recv_sem=rsem.at[i],
            device_id=to, device_id_type=MESH,
        )
        copy.start()
        started.append(copy)
        return copy

    started = []

    def done(until=None):
        for copy in started:
            copy.wait_send()

    zs = [dev(x, y, m4(z + d), c) for d in (1, 2, 3)]
    xs = [dev(m4(x + d), y, z, c) for d in (1, 2, 3)]
    x_flip = x_hi * 2 + 1 - x_lo
    hops = (0, 1, 2, 1)
    workers = [(d, e) for d in (0, 1) for e in range(4) if (d, e) != (0, 0)]
    workers.sort(key=lambda o: -(o[0] + hops[o[1]]))
    worker_of = lambda d, e: lax.rem(x_lo + d, 2) * 4 + m4(z + e)
    shards = [(d, h, k) for d in range(4) for h in (0, 1) for k in (0, 1) if (d, h, k) != (0, 0, 0)]
    shards.sort(key=lambda o: -(2 * hops[o[0]] + 4 * o[1] + o[2]))
    shard_of = lambda d, h, k: m4(y + d) * 4 + lax.rem(x_hi + h, 2) * 2 + lax.rem(c + k, 2)

    emb_copy = pltpu.make_async_copy(emb_hbm, emb, lsem.at[0])
    weight_copy = pltpu.make_async_copy(weight_hbm, WF.at[y, c], lsem.at[1])
    cot_copy = pltpu.make_async_copy(cot_hbm, cot, lsem.at[2])
    emb_copy.start()
    weight_copy.start()
    cot_copy.start()

    barrier = pltpu.get_barrier_semaphore()
    n_partners = 0
    for d, e in workers:
        pl.semaphore_signal(barrier, inc=1, device_id=(worker_of(d, e), s), device_id_type=MESH)
        n_partners += 1
    for o in shards:
        pl.semaphore_signal(barrier, inc=1, device_id=(w, shard_of(*o)), device_id_type=MESH)
        n_partners += 1
    pl.semaphore_signal(barrier, inc=1, device_id=dev(m4(x_flip + 2), y, z, c), device_id_type=MESH)
    n_partners += 1
    pl.semaphore_wait(barrier, n_partners)

    ids = ids_ref[...]
    ids_g[w] = jnp.broadcast_to(ids, (8, 256))
    first = [send(ids_g.at[w], ids_g.at[w], (worker_of(d, e), s)) for d, e in workers]

    cot_copy.wait()
    er, ec = iota((256, 256), 0), iota((256, 256), 1)
    idf = ids.astype(f32)
    id_row = jnp.broadcast_to(idf, (256, 256))
    id_col = jnp.sum(jnp.where(er == ec, id_row, 0.0), axis=1, keepdims=True)
    owner = ids >> 7
    own_row = jnp.broadcast_to(owner.astype(f32), (256, 256))
    own_col = jnp.sum(jnp.where(er == ec, own_row, 0.0), axis=1, keepdims=True)
    before = (own_col == own_row) & ((id_col < id_row) | ((id_col == id_row) & (er < ec)))
    rank = jnp.sum(jnp.where(before, 1.0, 0.0), axis=0, keepdims=True).astype(i32)
    turn_s = ((owner & 12) + ((owner & 1) << 1) + ((owner >> 1) & 1))
    place = turn_s * 16 + (owner >> 4) * 2 + rank
    cot_send[...] = dot(onehot(er == place), cot[...]).astype(bf16).reshape(cot_send.shape)
    x_pair = (w, y * 4 + (1 - x_hi) * 2 + c)
    s_pair = s + 2 - 4 * x_hi
    cot_x = [send(cot_send.at[0:3], cot_far.at[0:3], x_pair)]
    lines = [(d, k) for d in (2, 1, 3, 0) for k in (1, 0) if (d, k) != (0, 0)]
    pair_of = lambda d, k: m4(y + d) * 2 + lax.rem(c + k, 2)
    line_of = lambda d, k: (w, m4(y + d) * 4 + x_hi * 2 + lax.rem(c + k, 2))
    cots = [send(cot_send.at[pair_of(*o)], cot_recv.at[s], line_of(*o)) for o in lines]
    cot_recv[s] = cot_send[y * 2 + c]
    for copy in first:
        copy.wait_recv()
    row8 = iota((8, 256), 0)
    tile = ids_g[0]
    for i in range(1, 8):
        tile = jnp.where(row8 == i, ids_g[i], tile)
    ids_all[s] = tile
    second = [send(ids_all.at[s], ids_all.at[s], (w, shard_of(*o))) for o in shards]

    cot_x.append(send(cot_send.at[3:8], cot_far.at[3:8], x_pair))
    weight_copy.wait()
    fcol = jnp.full((1, 256), lax.rem(due_ref[0], 4), i32)
    due = [jnp.where(fcol == j, 1.0, 0.0) for j in range(4)]
    own_w = WF.at[y, c]
    frag = own_w[:, 0:256].astype(f32) * due[0]
    for j in range(1, 4):
        frag += own_w[:, j * 256:(j + 1) * 256].astype(f32) * due[j]
    fpad[rows:] = jnp.zeros((fpad.shape[0] - rows, 256), bf16)
    fpad[:rows] = frag.astype(bf16)
    eye = onehot(er == ec)
    f_send[...] = dot(eye, fpad[...], 1, 1).astype(bf16).reshape(f_send.shape)
    f_recv[w] = f_send[w]
    frags = [send(f_send.at[worker_of(d, e)], f_recv.at[w], (worker_of(d, e), s)) for d, e in workers]

    emb_copy.wait()
    n_rows = emb.shape[0]
    total = jnp.zeros((n_rows, 128), f32)

    def add_square(t, total):
        v = emb[:, pl.ds(pl.multiple_of(t * 128, 128), 128)].astype(f32)
        return total + v * v

    total = lax.fori_loop(0, width // 128, add_square, total, unroll=8)
    factor = lax.rsqrt(jnp.sum(total, axis=1, keepdims=True) / width + epsilon)

    def scale_rows(t, carry):
        at = pl.ds(pl.multiple_of(t * 128, 128), 128)
        normed[:, at] = (emb[:, at].astype(f32) * factor).astype(bf16)
        return carry

    lax.fori_loop(0, width // 128, scale_rows, 0, unroll=8)

    for copy in second:
        copy.wait_recv()

    me = w * 16 + s
    asked = ids_all[...].reshape(128, 256)
    local = (asked & 127).astype(f32)
    mine = (asked >> 7) == me
    low = jnp.min(jnp.where(mine, local, 999.0), axis=1, keepdims=True)
    high = jnp.max(jnp.where(mine, local, -1.0), axis=1, keepdims=True)
    r_out, r_in = iota((128, 128), 0), iota((128, 128), 1)
    turn = onehot(r_in == (r_out & 15) * 8 + (r_out >> 4))
    lane = iota((128, 128), 1).astype(f32)
    A, B = [], []
    for k, pick in ((0, low), (1, high)):
        sel = dot(turn, onehot(lane == pick)).astype(bf16)
        for q in range(8):
            got = dot(sel, normed[:, q * chunk:(q + 1) * chunk]).astype(bf16)
            yq, h = q // 2, q % 2
            for ww in range(8):
                xd, zd = h * 2 + ww // 4, ww % 4
                a, b = (zd, xd) if k == 0 else (xd, zd)
                SS[k, a, b, :, yq * chunk:(yq + 1) * chunk] = got[ww * 16:(ww + 1) * 16]
        for d in (1, 3, 2):
            if k == 0:
                A.append((d, send(SS.at[0, m4(z + d)], RA.at[z], dev(x, y, m4(z + d), c))))
            else:
                B.append((d, send(SS.at[1, m4(x + d)], RB.at[x], dev(m4(x + d), y, z, c))))

    arrive = []
    for d in (1, 3, 2):
        arrive.append(send(SS.at[0, z, m4(x + d)], N.at[x, z, 0], dev(m4(x + d), y, z, c)))
        arrive.append(send(SS.at[1, x, m4(z + d)], N.at[x, z, 1], dev(x, y, m4(z + d), c)))
    N[x, z, 0] = SS[0, z, x]
    N[x, z, 1] = SS[1, x, z]

    sib = (w, s + 1 - 2 * c)
    up, down = (w, m4(y + 1) * 4 + lax.rem(s, 4)), (w, m4(y + 3) * 4 + lax.rem(s, 4))
    w_up = send(WF.at[y, c], WF.at[y, c], up)
    w_down = send(WF.at[y, c], WF.at[y, c], down)
    w_sib = [send(WF.at[y, c], WF.at[y, c], sib)]

    for copy in cot_x:
        copy.wait_recv()
    cots += [send(cot_far.at[pair_of(*o)], cot_recv.at[s_pair], line_of(*o)) for o in lines]
    cot_recv[s_pair] = cot_far[y * 2 + c]
    for (d, a), (_, b) in zip(A, B):
        a.wait_recv()
        zf = m4(z - d)
        for e in (1, 3, 2):
            arrive.append(send(RA.at[zf, m4(x + e)], N.at[x, zf, 0], dev(m4(x + e), y, z, c)))
        N[x, zf, 0] = RA[zf, x]
        b.wait_recv()
        xf = m4(x - d)
        for e in (1, 3, 2):
            arrive.append(send(RB.at[xf, m4(z + e)], N.at[xf, z, 1], dev(x, y, m4(z + e), c)))
        N[xf, z, 1] = RB[xf, z]

    yu, yd = m4(y + 1), m4(y + 3)
    y2 = m4(y + 2)
    w_up.wait_recv()
    w_far_up = send(WF.at[yd, c, 0:hr], WF.at[yd, c, 0:hr], up)
    w_sib.append(send(WF.at[yd, c], WF.at[yd, c], sib))
    w_down.wait_recv()
    w_far_down = send(WF.at[yu, c, hr:rows], WF.at[yu, c, hr:rows], down)
    w_sib.append(send(WF.at[yu, c], WF.at[yu, c], sib))
    w_far_up.wait_recv()
    w_sib.append(send(WF.at[y2, c, 0:hr], WF.at[y2, c, 0:hr], sib))
    w_far_down.wait_recv()
    w_sib.append(send(WF.at[y2, c, hr:rows], WF.at[y2, c, hr:rows], sib))

    for copy in cots:
        copy.wait_recv()
    br, bc = iota((512, 512), 0), iota((512, 512), 1)
    back = onehot(bc == (br & 15) * 32 + (br >> 4))
    cot_rows[...] = dot(back, cot_recv[...].reshape(512, 1024)).astype(bf16)

    for copy in w_sib:
        copy.wait_recv()
    for copy in arrive:
        copy.wait_recv()

    px, core, far, near, written = {}, {}, {}, {}, []
    cols = lambda j: slice(starts[j], starts[j] + sizes[j])

    def forward(j):
        part = None
        for kk in range(4):
            a = N[:, :, :, :, kk * chunk:(kk + 1) * chunk].reshape(512, chunk)
            b = WF[kk, :, :, cols(j)].reshape(chunk, sizes[j])
            p = dot(a, b)
            part = p if part is None else part + p
        part = part * scale
        R["acc%d" % j][...] = part
        out, got = R["px_send%d" % j], R["px_recv%d" % j]
        out[...] = part.astype(bf16)
        px[j] = send(out, got, x_pair)

    def pointwise(j):
        px[j].wait_recv()
        pre = R["acc%d" % j][...] + R["px_recv%d" % j][...].astype(f32)
        sig = jax.nn.sigmoid(pre)
        g = cot_rows[:, cols(j)].astype(f32) * sig * (1.0 + pre * (1.0 - sig))
        R["G%d" % j][...] = g.astype(bf16)

    def turned():
        for q in range(half // 256):
            part = N[:, :, :, :, q * 256:(q + 1) * 256].reshape(512, 256)
            NT[q * 256:(q + 1) * 256] = dot(eye, part, 1, 1).astype(bf16)

    order = (2, 1, 3, 0)

    def backward(j):
        g = R["G%d" % j][...]
        CS, CR = R["CS%d" % j], R["CR%d" % j]
        for d in order:
            base = m4(y + d) * chunk
            other = NT[pl.ds(pl.multiple_of(base + (1 - c) * rows, 16), rows)]
            CS[d] = (dot(other, g) * scale).astype(bf16)
            core[j, d] = send(CS.at[d], CR.at[d], sib)
            own = NT[pl.ds(pl.multiple_of(base + c * rows, 16), rows)]
            PB[d, :, :sizes[j]] = dot(own, g) * scale

    def join(j):
        S2, SL, SR, R2, RL, RR = (R["%s%d" % (n, j)] for n in ("S2", "SL", "SR", "R2", "RL", "RR"))
        for d in order:
            core[j, d].wait_recv()
            t = PB[d, :, :sizes[j]] + R["CR%d" % j][d].astype(f32)
            if d == 2:
                S2[...] = t.astype(bf16)
                far[j] = (send(S2.at[0:hr], R2.at[0], up), send(S2.at[hr:rows], R2.at[1], down))
            elif d == 1:
                SL[hr:rows] = t[hr:rows].astype(bf16)
                near[j] = [send(SL.at[hr:rows], RL.at[hr:rows], up)]
                R["keep%d" % j][0] = t[0:hr]
            elif d == 3:
                SR[0:hr] = t[0:hr].astype(bf16)
                near[j].append(send(SR.at[0:hr], RR.at[0:hr], down))
                R["keep%d" % j][1] = t[hr:rows]
            else:
                R["own%d" % j][...] = t

    def pass_on(j):
        SL, SR, R2, RL, RR = (R["%s%d" % (n, j)] for n in ("SL", "SR", "R2", "RL", "RR"))
        far[j][0].wait_recv()
        SL[0:hr] = (R["keep%d" % j][0] + R2[0].astype(f32)).astype(bf16)
        near[j].append(send(SL.at[0:hr], RL.at[0:hr], up))
        far[j][1].wait_recv()
        SR[hr:rows] = (R["keep%d" % j][1] + R2[1].astype(f32)).astype(bf16)
        near[j].append(send(SR.at[hr:rows], RR.at[hr:rows], down))

    def finish(j):
        for copy in near[j]:
            copy.wait_recv()
        grads = R["own%d" % j][...] + R["RL%d" % j][...].astype(f32) + R["RR%d" % j][...].astype(f32)
        stepped = WF[y, c, :, cols(j)].astype(f32) - inner_rate * grads
        for p in range(0, sizes[j], 128):
            f, at = (starts[j] + p) // 256, (starts[j] + p) % 256
            share = due[f][:, :128] * (1.0 - mix_share)
            new = stepped[:, p:p + 128] * (1.0 - share) + share * full_anchor[:, at:at + 128]
            R["out%d" % j][:, p:p + 128] = new.astype(bf16)
        copy = pltpu.make_async_copy(R["out%d" % j], out_hbm.at[:, cols(j)], lsem.at[3 + j])
        copy.start()
        written.append(copy)

    def outer_update():
        for copy in frags:
            copy.wait_recv()
        mean = f_recv[0].astype(f32)
        for i in range(1, 8):
            mean += f_recv[i].astype(f32)
        mean = mean[:, :rows] / 8
        anchor = anchor_ref[...]
        delta = anchor - mean
        new_mom = outer_decay * mom_ref[...] + delta
        new_anchor = anchor - outer_rate * (delta + outer_decay * new_mom)
        new_mom_ref[...] = new_mom
        new_anchor_ref[...] = new_anchor
        a_send[:, rows:] = jnp.zeros((32, a_send.shape[1] - rows), bf16)
        a_send[:, :rows] = new_anchor.astype(bf16)
        anchors = [send(a_send, a_recv.at[w], (worker_of(d, e), s)) for d, e in workers]
        a_recv[w] = a_send[...]
        return anchors

    def outer_spread():
        for copy in anchors:
            copy.wait_recv()
        full_anchor[...] = dot(a_recv[...].reshape(256, 512), eye, 0, 0)[:rows]

    for j in range(n_cols):
        forward(j)
    turned()
    pointwise(0)
    backward(0)
    join(0)
    for j in range(1, n_cols):
        pointwise(j)
        backward(j)
        join(j)
        pass_on(j - 1)
        if j == 1:
            anchors = outer_update()
        if j == 3:
            outer_spread()
        if j >= 3:
            finish(j - 3)
    finish(n_cols - 3)
    pass_on(n_cols - 1)
    finish(n_cols - 2)
    finish(n_cols - 1)
    for copy in written:
        copy.wait()
    done()


def shards(token_ids, cotangent, embedding, weight, anchor, momentum, due_fragment):
    rows, width = weight.shape[1], embedding.shape[1]
    half = width // 2
    vmem = pl.BlockSpec(memory_space=pltpu.VMEM)
    anyspace = pl.BlockSpec(memory_space=pl.ANY)
    V, DMA = pltpu.VMEM, pltpu.SemaphoreType.DMA
    sizes = (128, 128, 256, 256, 128, 128)
    n_sends = 200
    scratch = {
        "emb": V((128, width), bf16),
        "normed": V((128, width), bf16),
        "cot": V((256, 1024), bf16),
        "ids_g": V((8, 8, 256), i32),
        "ids_all": V((16, 8, 256), i32),
        "SS": V((2, 4, 4, 16, half), bf16),
        "RA": V((4, 4, 16, half), bf16),
        "RB": V((4, 4, 16, half), bf16),
        "N": V((4, 4, 2, 16, half), bf16),
        "NT": V((half, 512), bf16),
        "WF": V((4, 2, rows, 1024), bf16),
        "cot_send": V((8, 32, 1024), bf16),
        "cot_far": V((8, 32, 1024), bf16),
        "cot_recv": V((16, 32, 1024), bf16),
        "cot_rows": V((512, 1024), bf16),
        "fpad": V((512, 256), bf16),
        "f_send": V((8, 32, 512), bf16),
        "f_recv": V((8, 32, 512), bf16),
        "a_send": V((32, 512), bf16),
        "a_recv": V((8, 32, 512), bf16),
        "full_anchor": V((rows, 256), f32),
        "PB": V((4, rows, 256), f32),
        "lsem": DMA((3 + len(sizes),)),
        "ssem": DMA((n_sends,)),
        "rsem": DMA((n_sends,)),
    }
    for j, n in enumerate(sizes):
        scratch["acc%d" % j] = V((512, n), f32)
        scratch["px_send%d" % j] = V((512, n), bf16)
        scratch["px_recv%d" % j] = V((512, n), bf16)
        scratch["G%d" % j] = V((512, n), bf16)
        scratch["keep%d" % j] = V((2, rows // 2, n), f32)
        scratch["CS%d" % j] = V((4, rows, n), bf16)
        scratch["CR%d" % j] = V((4, rows, n), bf16)
        scratch["R2%d" % j] = V((2, rows // 2, n), bf16)
        scratch["own%d" % j] = V((rows, n), f32)
        for name in ("S2", "SL", "SR", "RL", "RR", "out"):
            scratch["%s%d" % (name, j)] = V((rows, n), bf16)
    new_weight, new_anchor, new_momentum = pl.pallas_call(
        functools.partial(kernel, tuple(scratch), sizes),
        out_shape=(
            jax.ShapeDtypeStruct((rows, 1024), bf16),
            jax.ShapeDtypeStruct(anchor.shape[::-1], f32),
            jax.ShapeDtypeStruct(anchor.shape[::-1], f32),
        ),
        in_specs=[vmem, pl.BlockSpec(memory_space=pltpu.SMEM), vmem, vmem] + [anyspace] * 3,
        out_specs=(anyspace, vmem, vmem),
        scratch_shapes=list(scratch.values()),
        compiler_params=pltpu.CompilerParams(
            collective_id=0, has_side_effects=True, vmem_limit_bytes=60 * 2**20
        ),
        cost_estimate=pl.CostEstimate(flops=7_500_000_000, bytes_accessed=5_000_000, transcendentals=262144),
        name="diloco_step",
    )(token_ids.reshape(1, 256), due_fragment, anchor.T, momentum.T, embedding, weight.reshape(rows, 1024), cotangent)
    return (new_weight[None], new_anchor.T, new_momentum.T)


def solution(mesh):
    placed = (
        P(("worker", "shard")),
        P(("worker", "shard"), None),
        P(("worker", "shard"), None),
        P("worker", "shard", None),
        P("shard", "worker"),
        P("shard", "worker"),
        P(),
    )
    return jax.shard_map(
        shards,
        mesh=mesh,
        in_specs=placed,
        out_specs=(P("worker", "shard", None), P("shard", "worker"), P("shard", "worker")),
        check_vma=False,
    )
```

```python
import functools

import jax
import jax.numpy as jnp
from jax import lax
from jax.experimental import pallas as pl
from jax.experimental.pallas import tpu as pltpu
from jax.sharding import PartitionSpec as P

epsilon = 1e-06
inner_rate = 1.0
outer_rate = 0.7
outer_decay = 0.9
mix_share = 0.5

MESH = pl.DeviceIdType.MESH
f32, bf16, i32 = jnp.float32, jnp.bfloat16, jnp.int32


def iota(shape, dim):
    return lax.broadcasted_iota(i32, shape, dim)


def onehot(cond):
    return jnp.where(cond, 1.0, 0.0).astype(bf16)


def dot(a, b, ca=1, cb=0):
    return lax.dot_general(a, b, (((ca,), (cb,)), ((), ())), preferred_element_type=f32)


def m4(v):
    return lax.rem(v + 8, 4)


def kernel(
    names, sizes,
    ids_ref, due_ref, anchor_ref, mom_ref, emb_hbm, weight_hbm, cot_hbm,
    out_hbm, new_anchor_ref, new_mom_ref, *scratch,
):
    R = dict(zip(names, scratch))
    emb, normed, cot, ids_g, ids_all = (R[n] for n in ("emb", "normed", "cot", "ids_g", "ids_all"))
    SS, RA, RB, N, NT, WF = (R[n] for n in ("SS", "RA", "RB", "N", "NT", "WF"))
    cot_send, cot_far, cot_recv, cot_rows = (R[n] for n in ("cot_send", "cot_far", "cot_recv", "cot_rows"))
    fpad, f_send, f_recv = (R[n] for n in ("fpad", "f_send", "f_recv"))
    a_send, a_recv, full_anchor = (R[n] for n in ("a_send", "a_recv", "full_anchor"))
    PB = R["PB"]
    lsem, ssem, rsem = R["lsem"], R["ssem"], R["rsem"]
    n_cols = len(sizes)
    starts = [sum(sizes[:j]) for j in range(n_cols)]
    w = lax.axis_index("worker")
    s = lax.axis_index("shard")
    x_lo, z = w // 4, lax.rem(w, 4)
    y, x_hi, c = s // 4, lax.rem(s // 2, 2), lax.rem(s, 2)
    x = x_hi * 2 + x_lo
    width = emb.shape[1]
    half = width // 2
    chunk = width // 8
    scale = width ** (-0.5)
    rows = WF.shape[2]
    hr = rows // 2

    def dev(xx, yy, zz, cc):
        return (lax.rem(xx, 2) * 4 + zz, yy * 4 + (xx // 2) * 2 + cc)

    counter = [0]

    def send(src, dst, to):
        i = counter[0]
        counter[0] += 1
        copy = pltpu.make_async_remote_copy(
            src_ref=src, dst_ref=dst, send_sem=ssem.at[i], recv_sem=rsem.at[i],
            device_id=to, device_id_type=MESH,
        )
        copy.start()
        started.append(copy)
        return copy

    started = []

    def done(until=None):
        for copy in started:
            copy.wait_send()

    zs = [dev(x, y, m4(z + d), c) for d in (1, 2, 3)]
    xs = [dev(m4(x + d), y, z, c) for d in (1, 2, 3)]
    x_flip = x_hi * 2 + 1 - x_lo
    hops = (0, 1, 2, 1)
    workers = [(d, e) for d in (0, 1) for e in range(4) if (d, e) != (0, 0)]
    workers.sort(key=lambda o: -(o[0] + hops[o[1]]))
    worker_of = lambda d, e: lax.rem(x_lo + d, 2) * 4 + m4(z + e)
    shards = [(d, h, k) for d in range(4) for h in (0, 1) for k in (0, 1) if (d, h, k) != (0, 0, 0)]
    shards.sort(key=lambda o: -(2 * hops[o[0]] + 4 * o[1] + o[2]))
    shard_of = lambda d, h, k: m4(y + d) * 4 + lax.rem(x_hi + h, 2) * 2 + lax.rem(c + k, 2)

    emb_copy = pltpu.make_async_copy(emb_hbm, emb, lsem.at[0])
    weight_copy = pltpu.make_async_copy(weight_hbm, WF.at[y, c], lsem.at[1])
    cot_copy = pltpu.make_async_copy(cot_hbm, cot, lsem.at[2])
    emb_copy.start()
    weight_copy.start()
    cot_copy.start()

    barrier = pltpu.get_barrier_semaphore()
    n_partners = 0
    for d, e in workers:
        pl.semaphore_signal(barrier, inc=1, device_id=(worker_of(d, e), s), device_id_type=MESH)
        n_partners += 1
    for o in shards:
        pl.semaphore_signal(barrier, inc=1, device_id=(w, shard_of(*o)), device_id_type=MESH)
        n_partners += 1
    pl.semaphore_signal(barrier, inc=1, device_id=dev(m4(x_flip + 2), y, z, c), device_id_type=MESH)
    n_partners += 1
    pl.semaphore_wait(barrier, n_partners)

    ids = ids_ref[...]
    ids_g[w] = jnp.broadcast_to(ids, (8, 256))
    first = [send(ids_g.at[w], ids_g.at[w], (worker_of(d, e), s)) for d, e in workers]

    cot_copy.wait()
    er, ec = iota((256, 256), 0), iota((256, 256), 1)
    idf = ids.astype(f32)
    id_row = jnp.broadcast_to(idf, (256, 256))
    id_col = jnp.sum(jnp.where(er == ec, id_row, 0.0), axis=1, keepdims=True)
    owner = ids >> 7
    own_row = jnp.broadcast_to(owner.astype(f32), (256, 256))
    own_col = jnp.sum(jnp.where(er == ec, own_row, 0.0), axis=1, keepdims=True)
    before = (own_col == own_row) & ((id_col < id_row) | ((id_col == id_row) & (er < ec)))
    rank = jnp.sum(jnp.where(before, 1.0, 0.0), axis=0, keepdims=True).astype(i32)
    turn_s = ((owner & 12) + ((owner & 1) << 1) + ((owner >> 1) & 1))
    place = turn_s * 16 + (owner >> 4) * 2 + rank
    cot_send[...] = dot(onehot(er == place), cot[...]).astype(bf16).reshape(cot_send.shape)
    x_pair = (w, y * 4 + (1 - x_hi) * 2 + c)
    s_pair = s + 2 - 4 * x_hi
    cot_x = [send(cot_send.at[0:4], cot_far.at[0:4], x_pair)]
    lines = [(d, k) for d in (2, 1, 3, 0) for k in (1, 0) if (d, k) != (0, 0)]
    pair_of = lambda d, k: m4(y + d) * 2 + lax.rem(c + k, 2)
    line_of = lambda d, k: (w, m4(y + d) * 4 + x_hi * 2 + lax.rem(c + k, 2))
    cots = [send(cot_send.at[pair_of(*o)], cot_recv.at[s], line_of(*o)) for o in lines]
    cot_recv[s] = cot_send[y * 2 + c]
    for copy in first:
        copy.wait_recv()
    row8 = iota((8, 256), 0)
    tile = ids_g[0]
    for i in range(1, 8):
        tile = jnp.where(row8 == i, ids_g[i], tile)
    ids_all[s] = tile
    second = [send(ids_all.at[s], ids_all.at[s], (w, shard_of(*o))) for o in shards]

    cot_x.append(send(cot_send.at[4:8], cot_far.at[4:8], x_pair))
    weight_copy.wait()
    sib = (w, s + 1 - 2 * c)
    up, down = (w, m4(y + 1) * 4 + lax.rem(s, 4)), (w, m4(y + 3) * 4 + lax.rem(s, 4))
    w_up = send(WF.at[y, c], WF.at[y, c], up)
    w_down = send(WF.at[y, c], WF.at[y, c], down)
    w_sib = [send(WF.at[y, c], WF.at[y, c], sib)]

    fcol = jnp.full((1, 256), lax.rem(due_ref[0], 4), i32)
    due = [jnp.where(fcol == j, 1.0, 0.0) for j in range(4)]
    own_w = WF.at[y, c]
    frag = own_w[:, 0:256].astype(f32) * due[0]
    for j in range(1, 4):
        frag += own_w[:, j * 256:(j + 1) * 256].astype(f32) * due[j]
    fpad[rows:] = jnp.zeros((fpad.shape[0] - rows, 256), bf16)
    fpad[:rows] = frag.astype(bf16)
    eye = onehot(er == ec)
    f_send[...] = dot(eye, fpad[...], 1, 1).astype(bf16).reshape(f_send.shape)
    f_recv[w] = f_send[w]

    emb_copy.wait()
    n_rows = emb.shape[0]
    total = jnp.zeros((n_rows, 128), f32)

    def add_square(t, total):
        v = emb[:, pl.ds(pl.multiple_of(t * 128, 128), 128)].astype(f32)
        return total + v * v

    total = lax.fori_loop(0, width // 128, add_square, total, unroll=8)
    factor = lax.rsqrt(jnp.sum(total, axis=1, keepdims=True) / width + epsilon)

    def scale_rows(t, carry):
        at = pl.ds(pl.multiple_of(t * 128, 128), 128)
        normed[:, at] = (emb[:, at].astype(f32) * factor).astype(bf16)
        return carry

    lax.fori_loop(0, width // 128, scale_rows, 0, unroll=8)

    for copy in second:
        copy.wait_recv()

    me = w * 16 + s
    asked = ids_all[...].reshape(128, 256)
    local = (asked & 127).astype(f32)
    mine = (asked >> 7) == me
    low = jnp.min(jnp.where(mine, local, 999.0), axis=1, keepdims=True)
    high = jnp.max(jnp.where(mine, local, -1.0), axis=1, keepdims=True)
    r_out, r_in = iota((128, 128), 0), iota((128, 128), 1)
    turn = onehot(r_in == (r_out & 15) * 8 + (r_out >> 4))
    lane = iota((128, 128), 1).astype(f32)
    A, B = [], []
    for k, pick in ((0, low), (1, high)):
        sel = dot(turn, onehot(lane == pick)).astype(bf16)
        for q in range(8):
            got = dot(sel, normed[:, q * chunk:(q + 1) * chunk]).astype(bf16)
            yq, h = q // 2, q % 2
            for ww in range(8):
                xd, zd = h * 2 + ww // 4, ww % 4
                a, b = (zd, xd) if k == 0 else (xd, zd)
                SS[k, a, b, :, yq * chunk:(yq + 1) * chunk] = got[ww * 16:(ww + 1) * 16]
        for d in (1, 3, 2):
            if k == 0:
                A.append((d, send(SS.at[0, m4(z + d)], RA.at[z], dev(x, y, m4(z + d), c))))
            else:
                B.append((d, send(SS.at[1, m4(x + d)], RB.at[x], dev(m4(x + d), y, z, c))))

    arrive = []
    for d in (1, 3, 2):
        arrive.append(send(SS.at[0, z, m4(x + d)], N.at[x, z, 0], dev(m4(x + d), y, z, c)))
        arrive.append(send(SS.at[1, x, m4(z + d)], N.at[x, z, 1], dev(x, y, m4(z + d), c)))
    N[x, z, 0] = SS[0, z, x]
    N[x, z, 1] = SS[1, x, z]

    for copy in cot_x:
        copy.wait_recv()
    cots += [send(cot_far.at[pair_of(*o)], cot_recv.at[s_pair], line_of(*o)) for o in lines]
    cot_recv[s_pair] = cot_far[y * 2 + c]
    for (d, a), (_, b) in zip(A, B):
        a.wait_recv()
        zf = m4(z - d)
        for e in (1, 3, 2):
            arrive.append(send(RA.at[zf, m4(x + e)], N.at[x, zf, 0], dev(m4(x + e), y, z, c)))
        N[x, zf, 0] = RA[zf, x]
        b.wait_recv()
        xf = m4(x - d)
        for e in (1, 3, 2):
            arrive.append(send(RB.at[xf, m4(z + e)], N.at[xf, z, 1], dev(x, y, m4(z + e), c)))
        N[xf, z, 1] = RB[xf, z]

    yu, yd = m4(y + 1), m4(y + 3)
    y2 = m4(y + 2)
    w_up.wait_recv()
    w_far_up = send(WF.at[yd, c, 0:hr], WF.at[yd, c, 0:hr], up)
    w_sib.append(send(WF.at[yd, c], WF.at[yd, c], sib))
    w_down.wait_recv()
    w_far_down = send(WF.at[yu, c, hr:rows], WF.at[yu, c, hr:rows], down)
    w_sib.append(send(WF.at[yu, c], WF.at[yu, c], sib))
    w_far_up.wait_recv()
    w_sib.append(send(WF.at[y2, c, 0:hr], WF.at[y2, c, 0:hr], sib))
    w_far_down.wait_recv()
    w_sib.append(send(WF.at[y2, c, hr:rows], WF.at[y2, c, hr:rows], sib))

    for copy in cots:
        copy.wait_recv()
    br, bc = iota((512, 512), 0), iota((512, 512), 1)
    back = onehot(bc == (br & 15) * 32 + (br >> 4))
    cot_rows[...] = dot(back, cot_recv[...].reshape(512, 1024)).astype(bf16)

    for copy in w_sib:
        copy.wait_recv()
    for copy in arrive:
        copy.wait_recv()

    px, core, far, near, written = {}, {}, {}, {}, []
    cols = lambda j: slice(starts[j], starts[j] + sizes[j])

    def forward(j):
        part = None
        for kk in range(4):
            a = N[:, :, :, :, kk * chunk:(kk + 1) * chunk].reshape(512, chunk)
            b = WF[kk, :, :, cols(j)].reshape(chunk, sizes[j])
            p = dot(a, b)
            part = p if part is None else part + p
        part = part * scale
        R["acc%d" % j][...] = part
        out, got = R["px_send%d" % j], R["px_recv%d" % j]
        out[...] = part.astype(bf16)
        px[j] = send(out, got, x_pair)

    def pointwise(j):
        px[j].wait_recv()
        pre = R["acc%d" % j][...] + R["px_recv%d" % j][...].astype(f32)
        sig = jax.nn.sigmoid(pre)
        g = cot_rows[:, cols(j)].astype(f32) * sig * (1.0 + pre * (1.0 - sig))
        R["G%d" % j][...] = g.astype(bf16)

    def turned():
        for q in range(half // 256):
            part = N[:, :, :, :, q * 256:(q + 1) * 256].reshape(512, 256)
            NT[q * 256:(q + 1) * 256] = dot(eye, part, 1, 1).astype(bf16)

    order = (2, 1, 3, 0)

    def backward(j):
        g = R["G%d" % j][...]
        CS, CR = R["CS%d" % j], R["CR%d" % j]
        for d in order:
            base = m4(y + d) * chunk
            other = NT[pl.ds(pl.multiple_of(base + (1 - c) * rows, 16), rows)]
            CS[d] = (dot(other, g) * scale).astype(bf16)
            core[j, d] = send(CS.at[d], CR.at[d], sib)
            own = NT[pl.ds(pl.multiple_of(base + c * rows, 16), rows)]
            PB[d, :, :sizes[j]] = dot(own, g) * scale

    def join(j):
        S2, SL, SR, R2, RL, RR = (R["%s%d" % (n, j)] for n in ("S2", "SL", "SR", "R2", "RL", "RR"))
        for d in order:
            core[j, d].wait_recv()
            t = PB[d, :, :sizes[j]] + R["CR%d" % j][d].astype(f32)
            if d == 2:
                S2[...] = t.astype(bf16)
                far[j] = (send(S2.at[0:hr], R2.at[0], up), send(S2.at[hr:rows], R2.at[1], down))
            elif d == 1:
                SL[hr:rows] = t[hr:rows].astype(bf16)
                near[j] = [send(SL.at[hr:rows], RL.at[hr:rows], up)]
                R["keep%d" % j][0] = t[0:hr]
            elif d == 3:
                SR[0:hr] = t[0:hr].astype(bf16)
                near[j].append(send(SR.at[0:hr], RR.at[0:hr], down))
                R["keep%d" % j][1] = t[hr:rows]
            else:
                R["own%d" % j][...] = t

    def pass_on(j):
        SL, SR, R2, RL, RR = (R["%s%d" % (n, j)] for n in ("SL", "SR", "R2", "RL", "RR"))
        far[j][0].wait_recv()
        SL[0:hr] = (R["keep%d" % j][0] + R2[0].astype(f32)).astype(bf16)
        near[j].append(send(SL.at[0:hr], RL.at[0:hr], up))
        far[j][1].wait_recv()
        SR[hr:rows] = (R["keep%d" % j][1] + R2[1].astype(f32)).astype(bf16)
        near[j].append(send(SR.at[hr:rows], RR.at[hr:rows], down))

    def finish(j):
        for copy in near[j]:
            copy.wait_recv()
        grads = R["own%d" % j][...] + R["RL%d" % j][...].astype(f32) + R["RR%d" % j][...].astype(f32)
        stepped = WF[y, c, :, cols(j)].astype(f32) - inner_rate * grads
        for p in range(0, sizes[j], 128):
            f, at = (starts[j] + p) // 256, (starts[j] + p) % 256
            share = due[f][:, :128] * (1.0 - mix_share)
            new = stepped[:, p:p + 128] * (1.0 - share) + share * full_anchor[:, at:at + 128]
            R["out%d" % j][:, p:p + 128] = new.astype(bf16)
        copy = pltpu.make_async_copy(R["out%d" % j], out_hbm.at[:, cols(j)], lsem.at[3 + j])
        copy.start()
        written.append(copy)

    def outer_update():
        for copy in frags:
            copy.wait_recv()
        mean = f_recv[0].astype(f32)
        for i in range(1, 8):
            mean += f_recv[i].astype(f32)
        mean = mean[:, :rows] / 8
        anchor = anchor_ref[...]
        delta = anchor - mean
        new_mom = outer_decay * mom_ref[...] + delta
        new_anchor = anchor - outer_rate * (delta + outer_decay * new_mom)
        new_mom_ref[...] = new_mom
        new_anchor_ref[...] = new_anchor
        a_send[:, rows:] = jnp.zeros((32, a_send.shape[1] - rows), bf16)
        a_send[:, :rows] = new_anchor.astype(bf16)
        anchors = [send(a_send, a_recv.at[w], (worker_of(d, e), s)) for d, e in workers]
        a_recv[w] = a_send[...]
        return anchors

    def outer_spread():
        for copy in anchors:
            copy.wait_recv()
        full_anchor[...] = dot(a_recv[...].reshape(256, 512), eye, 0, 0)[:rows]

    for j in range(n_cols):
        forward(j)
    frags = [send(f_send.at[worker_of(d, e)], f_recv.at[w], (worker_of(d, e), s)) for d, e in workers]
    turned()
    pointwise(0)
    backward(0)
    join(0)
    for j in range(1, n_cols):
        pointwise(j)
        backward(j)
        join(j)
        pass_on(j - 1)
        if j == n_cols - 2:
            anchors = outer_update()
    outer_spread()
    for j in range(n_cols - 3):
        finish(j)
    pass_on(n_cols - 1)
    for j in range(n_cols - 3, n_cols):
        finish(j)
    for copy in written:
        copy.wait()
    done()


def shards(token_ids, cotangent, embedding, weight, anchor, momentum, due_fragment):
    rows, width = weight.shape[1], embedding.shape[1]
    half = width // 2
    vmem = pl.BlockSpec(memory_space=pltpu.VMEM)
    anyspace = pl.BlockSpec(memory_space=pl.ANY)
    V, DMA = pltpu.VMEM, pltpu.SemaphoreType.DMA
    sizes = (128, 128, 256, 256, 128, 128)
    n_sends = 200
    scratch = {
        "emb": V((128, width), bf16),
        "normed": V((128, width), bf16),
        "cot": V((256, 1024), bf16),
        "ids_g": V((8, 8, 256), i32),
        "ids_all": V((16, 8, 256), i32),
        "SS": V((2, 4, 4, 16, half), bf16),
        "RA": V((4, 4, 16, half), bf16),
        "RB": V((4, 4, 16, half), bf16),
        "N": V((4, 4, 2, 16, half), bf16),
        "NT": V((half, 512), bf16),
        "WF": V((4, 2, rows, 1024), bf16),
        "cot_send": V((8, 32, 1024), bf16),
        "cot_far": V((8, 32, 1024), bf16),
        "cot_recv": V((16, 32, 1024), bf16),
        "cot_rows": V((512, 1024), bf16),
        "fpad": V((512, 256), bf16),
        "f_send": V((8, 32, 512), bf16),
        "f_recv": V((8, 32, 512), bf16),
        "a_send": V((32, 512), bf16),
        "a_recv": V((8, 32, 512), bf16),
        "full_anchor": V((rows, 256), f32),
        "PB": V((4, rows, 256), f32),
        "lsem": DMA((3 + len(sizes),)),
        "ssem": DMA((n_sends,)),
        "rsem": DMA((n_sends,)),
    }
    for j, n in enumerate(sizes):
        scratch["acc%d" % j] = V((512, n), f32)
        scratch["px_send%d" % j] = V((512, n), bf16)
        scratch["px_recv%d" % j] = V((512, n), bf16)
        scratch["G%d" % j] = V((512, n), bf16)
        scratch["keep%d" % j] = V((2, rows // 2, n), f32)
        scratch["CS%d" % j] = V((4, rows, n), bf16)
        scratch["CR%d" % j] = V((4, rows, n), bf16)
        scratch["R2%d" % j] = V((2, rows // 2, n), bf16)
        scratch["own%d" % j] = V((rows, n), f32)
        for name in ("S2", "SL", "SR", "RL", "RR", "out"):
            scratch["%s%d" % (name, j)] = V((rows, n), bf16)
    new_weight, new_anchor, new_momentum = pl.pallas_call(
        functools.partial(kernel, tuple(scratch), sizes),
        out_shape=(
            jax.ShapeDtypeStruct((rows, 1024), bf16),
            jax.ShapeDtypeStruct(anchor.shape[::-1], f32),
            jax.ShapeDtypeStruct(anchor.shape[::-1], f32),
        ),
        in_specs=[vmem, pl.BlockSpec(memory_space=pltpu.SMEM), vmem, vmem] + [anyspace] * 3,
        out_specs=(anyspace, vmem, vmem),
        scratch_shapes=list(scratch.values()),
        compiler_params=pltpu.CompilerParams(
            collective_id=0, has_side_effects=True, vmem_limit_bytes=60 * 2**20
        ),
        cost_estimate=pl.CostEstimate(flops=7_500_000_000, bytes_accessed=5_000_000, transcendentals=262144),
        name="diloco_step",
    )(token_ids.reshape(1, 256), due_fragment, anchor.T, momentum.T, embedding, weight.reshape(rows, 1024), cotangent)
    return (new_weight[None], new_anchor.T, new_momentum.T)


def solution(mesh):
    placed = (
        P(("worker", "shard")),
        P(("worker", "shard"), None),
        P(("worker", "shard"), None),
        P("worker", "shard", None),
        P("shard", "worker"),
        P("shard", "worker"),
        P(),
    )
    return jax.shard_map(
        shards,
        mesh=mesh,
        in_specs=placed,
        out_specs=(P("worker", "shard", None), P("shard", "worker"), P("shard", "worker")),
        check_vma=False,
    )
```

```python
import functools

import jax
import jax.numpy as jnp
from jax import lax
from jax.experimental import pallas as pl
from jax.experimental.pallas import tpu as pltpu
from jax.sharding import PartitionSpec as P

epsilon = 1e-06
inner_rate = 1.0
outer_rate = 0.7
outer_decay = 0.9
mix_share = 0.5

MESH = pl.DeviceIdType.MESH
f32, bf16, i32 = jnp.float32, jnp.bfloat16, jnp.int32


def iota(shape, dim):
    return lax.broadcasted_iota(i32, shape, dim)


def onehot(cond):
    return jnp.where(cond, 1.0, 0.0).astype(bf16)


def dot(a, b, ca=1, cb=0):
    return lax.dot_general(a, b, (((ca,), (cb,)), ((), ())), preferred_element_type=f32)


def m4(v):
    return lax.rem(v + 8, 4)


def kernel(
    names, sizes,
    ids_hbm, due_hbm, anchor_hbm, mom_hbm, emb_hbm, weight_hbm, cot_hbm,
    out_hbm, new_anchor_hbm, new_mom_hbm, *scratch,
):
    R = dict(zip(names, scratch))
    emb, normed, cot, ids_g, ids_all = (R[n] for n in ("emb", "normed", "cot", "ids_g", "ids_all"))
    SS, RA, RB, N, NT, WF = (R[n] for n in ("SS", "RA", "RB", "N", "NT", "WF"))
    cot_send, cot_far, cot_recv, cot_rows = (R[n] for n in ("cot_send", "cot_far", "cot_recv", "cot_rows"))
    fpad, f_send, f_recv = (R[n] for n in ("fpad", "f_send", "f_recv"))
    a_send, a_recv, full_anchor = (R[n] for n in ("a_send", "a_recv", "full_anchor"))
    PB = R["PB"]
    small = ("ids", "due", "anchor", "mom", "new_anchor", "new_mom")
    ids_ref, due_ref, anchor_ref, mom_ref, new_anchor_ref, new_mom_ref = (R[n] for n in small)
    lsem, ssem, rsem = R["lsem"], R["ssem"], R["rsem"]
    n_cols = len(sizes)
    starts = [sum(sizes[:j]) for j in range(n_cols)]
    w = lax.axis_index("worker")
    s = lax.axis_index("shard")
    x_lo, z = w // 4, lax.rem(w, 4)
    y, x_hi, c = s // 4, lax.rem(s // 2, 2), lax.rem(s, 2)
    x = x_hi * 2 + x_lo
    width = emb.shape[1]
    half = width // 2
    chunk = width // 8
    scale = width ** (-0.5)
    rows = WF.shape[2]
    hr = rows // 2

    def dev(xx, yy, zz, cc):
        return (lax.rem(xx, 2) * 4 + zz, yy * 4 + (xx // 2) * 2 + cc)

    counter = [0]

    def send(src, dst, to):
        i = counter[0]
        counter[0] += 1
        copy = pltpu.make_async_remote_copy(
            src_ref=src, dst_ref=dst, send_sem=ssem.at[i], recv_sem=rsem.at[i],
            device_id=to, device_id_type=MESH,
        )
        copy.start()
        started.append(copy)
        return copy

    started = []

    def done(until=None):
        for copy in started:
            copy.wait_send()

    zs = [dev(x, y, m4(z + d), c) for d in (1, 2, 3)]
    xs = [dev(m4(x + d), y, z, c) for d in (1, 2, 3)]
    x_flip = x_hi * 2 + 1 - x_lo
    hops = (0, 1, 2, 1)
    workers = [(d, e) for d in (0, 1) for e in range(4) if (d, e) != (0, 0)]
    workers.sort(key=lambda o: -(o[0] + hops[o[1]]))
    worker_of = lambda d, e: lax.rem(x_lo + d, 2) * 4 + m4(z + e)
    shards = [(d, h, k) for d in range(4) for h in (0, 1) for k in (0, 1) if (d, h, k) != (0, 0, 0)]
    shards.sort(key=lambda o: -(2 * hops[o[0]] + 4 * o[1] + o[2]))
    shard_of = lambda d, h, k: m4(y + d) * 4 + lax.rem(x_hi + h, 2) * 2 + lax.rem(c + k, 2)

    emb_copy = pltpu.make_async_copy(emb_hbm, emb, lsem.at[0])
    weight_copy = pltpu.make_async_copy(weight_hbm, WF.at[y, c], lsem.at[1])
    cot_copy = pltpu.make_async_copy(cot_hbm, cot, lsem.at[2])
    at_small = 3 + n_cols
    small_in = [
        pltpu.make_async_copy(src, dst, lsem.at[at_small + i])
        for i, (src, dst) in enumerate(
            ((ids_hbm, ids_ref), (due_hbm, due_ref), (anchor_hbm, anchor_ref), (mom_hbm, mom_ref))
        )
    ]
    for copy in small_in:
        copy.start()
    emb_copy.start()
    weight_copy.start()
    cot_copy.start()

    barrier = pltpu.get_barrier_semaphore()
    n_partners = 0
    for d, e in workers:
        pl.semaphore_signal(barrier, inc=1, device_id=(worker_of(d, e), s), device_id_type=MESH)
        n_partners += 1
    for o in shards:
        pl.semaphore_signal(barrier, inc=1, device_id=(w, shard_of(*o)), device_id_type=MESH)
        n_partners += 1
    pl.semaphore_signal(barrier, inc=1, device_id=dev(m4(x_flip + 2), y, z, c), device_id_type=MESH)
    n_partners += 1
    pl.semaphore_wait(barrier, n_partners)

    small_in[0].wait()
    ids = ids_ref[...]
    ids_g[w] = jnp.broadcast_to(ids, (8, 256))
    first = [send(ids_g.at[w], ids_g.at[w], (worker_of(d, e), s)) for d, e in workers]

    cot_copy.wait()
    er, ec = iota((256, 256), 0), iota((256, 256), 1)
    idf = ids.astype(f32)
    id_row = jnp.broadcast_to(idf, (256, 256))
    id_col = jnp.sum(jnp.where(er == ec, id_row, 0.0), axis=1, keepdims=True)
    owner = ids >> 7
    own_row = jnp.broadcast_to(owner.astype(f32), (256, 256))
    own_col = jnp.sum(jnp.where(er == ec, own_row, 0.0), axis=1, keepdims=True)
    before = (own_col == own_row) & ((id_col < id_row) | ((id_col == id_row) & (er < ec)))
    rank = jnp.sum(jnp.where(before, 1.0, 0.0), axis=0, keepdims=True).astype(i32)
    turn_s = ((owner & 12) + ((owner & 1) << 1) + ((owner >> 1) & 1))
    place = turn_s * 16 + (owner >> 4) * 2 + rank
    cot_send[...] = dot(onehot(er == place), cot[...]).astype(bf16).reshape(cot_send.shape)
    x_pair = (w, y * 4 + (1 - x_hi) * 2 + c)
    s_pair = s + 2 - 4 * x_hi
    cot_x = [send(cot_send.at[0:4], cot_far.at[0:4], x_pair)]
    lines = [(d, k) for d in (2, 1, 3, 0) for k in (1, 0) if (d, k) != (0, 0)]
    pair_of = lambda d, k: m4(y + d) * 2 + lax.rem(c + k, 2)
    line_of = lambda d, k: (w, m4(y + d) * 4 + x_hi * 2 + lax.rem(c + k, 2))
    cots = [send(cot_send.at[pair_of(*o)], cot_recv.at[s], line_of(*o)) for o in lines]
    cot_recv[s] = cot_send[y * 2 + c]
    for copy in first:
        copy.wait_recv()
    row8 = iota((8, 256), 0)
    tile = ids_g[0]
    for i in range(1, 8):
        tile = jnp.where(row8 == i, ids_g[i], tile)
    ids_all[s] = tile
    second = [send(ids_all.at[s], ids_all.at[s], (w, shard_of(*o))) for o in shards]

    cot_x.append(send(cot_send.at[4:8], cot_far.at[4:8], x_pair))
    weight_copy.wait()
    sib = (w, s + 1 - 2 * c)
    up, down = (w, m4(y + 1) * 4 + lax.rem(s, 4)), (w, m4(y + 3) * 4 + lax.rem(s, 4))
    w_up = send(WF.at[y, c], WF.at[y, c], up)
    w_down = send(WF.at[y, c], WF.at[y, c], down)
    w_sib = [send(WF.at[y, c], WF.at[y, c], sib)]

    for copy in small_in[1:]:
        copy.wait()
    fcol = jnp.full((1, 256), lax.rem(due_ref[0], 4), i32)
    due = [jnp.where(fcol == j, 1.0, 0.0) for j in range(4)]
    own_w = WF.at[y, c]
    frag = own_w[:, 0:256].astype(f32) * due[0]
    for j in range(1, 4):
        frag += own_w[:, j * 256:(j + 1) * 256].astype(f32) * due[j]
    fpad[rows:] = jnp.zeros((fpad.shape[0] - rows, 256), bf16)
    fpad[:rows] = frag.astype(bf16)
    eye = onehot(er == ec)
    f_send[...] = dot(eye, fpad[...], 1, 1).astype(bf16).reshape(f_send.shape)
    f_recv[w] = f_send[w]

    emb_copy.wait()
    n_rows = emb.shape[0]
    total = jnp.zeros((n_rows, 128), f32)

    def add_square(t, total):
        v = emb[:, pl.ds(pl.multiple_of(t * 128, 128), 128)].astype(f32)
        return total + v * v

    total = lax.fori_loop(0, width // 128, add_square, total, unroll=8)
    factor = lax.rsqrt(jnp.sum(total, axis=1, keepdims=True) / width + epsilon)

    def scale_rows(t, carry):
        at = pl.ds(pl.multiple_of(t * 128, 128), 128)
        normed[:, at] = (emb[:, at].astype(f32) * factor).astype(bf16)
        return carry

    lax.fori_loop(0, width // 128, scale_rows, 0, unroll=8)

    for copy in second:
        copy.wait_recv()

    me = w * 16 + s
    asked = ids_all[...].reshape(128, 256)
    local = (asked & 127).astype(f32)
    mine = (asked >> 7) == me
    low = jnp.min(jnp.where(mine, local, 999.0), axis=1, keepdims=True)
    high = jnp.max(jnp.where(mine, local, -1.0), axis=1, keepdims=True)
    r_out, r_in = iota((128, 128), 0), iota((128, 128), 1)
    turn = onehot(r_in == (r_out & 15) * 8 + (r_out >> 4))
    lane = iota((128, 128), 1).astype(f32)
    A, B = [], []
    for k, pick in ((0, low), (1, high)):
        sel = dot(turn, onehot(lane == pick)).astype(bf16)
        for q in range(8):
            got = dot(sel, normed[:, q * chunk:(q + 1) * chunk]).astype(bf16)
            yq, h = q // 2, q % 2
            for ww in range(8):
                xd, zd = h * 2 + ww // 4, ww % 4
                a, b = (zd, xd) if k == 0 else (xd, zd)
                SS[k, a, b, :, yq * chunk:(yq + 1) * chunk] = got[ww * 16:(ww + 1) * 16]
        for d in (1, 3, 2):
            if k == 0:
                A.append((d, send(SS.at[0, m4(z + d)], RA.at[z], dev(x, y, m4(z + d), c))))
            else:
                B.append((d, send(SS.at[1, m4(x + d)], RB.at[x], dev(m4(x + d), y, z, c))))

    arrive = []
    for d in (1, 3, 2):
        arrive.append(send(SS.at[0, z, m4(x + d)], N.at[x, z, 0], dev(m4(x + d), y, z, c)))
        arrive.append(send(SS.at[1, x, m4(z + d)], N.at[x, z, 1], dev(x, y, m4(z + d), c)))
    N[x, z, 0] = SS[0, z, x]
    N[x, z, 1] = SS[1, x, z]

    for copy in cot_x:
        copy.wait_recv()
    cots += [send(cot_far.at[pair_of(*o)], cot_recv.at[s_pair], line_of(*o)) for o in lines]
    cot_recv[s_pair] = cot_far[y * 2 + c]
    for (d, a), (_, b) in zip(A, B):
        a.wait_recv()
        zf = m4(z - d)
        for e in (1, 3, 2):
            arrive.append(send(RA.at[zf, m4(x + e)], N.at[x, zf, 0], dev(m4(x + e), y, z, c)))
        N[x, zf, 0] = RA[zf, x]
        b.wait_recv()
        xf = m4(x - d)
        for e in (1, 3, 2):
            arrive.append(send(RB.at[xf, m4(z + e)], N.at[xf, z, 1], dev(x, y, m4(z + e), c)))
        N[xf, z, 1] = RB[xf, z]

    yu, yd = m4(y + 1), m4(y + 3)
    y2 = m4(y + 2)
    w_up.wait_recv()
    w_far_up = send(WF.at[yd, c, 0:hr], WF.at[yd, c, 0:hr], up)
    w_sib.append(send(WF.at[yd, c], WF.at[yd, c], sib))
    w_down.wait_recv()
    w_far_down = send(WF.at[yu, c, hr:rows], WF.at[yu, c, hr:rows], down)
    w_sib.append(send(WF.at[yu, c], WF.at[yu, c], sib))
    w_far_up.wait_recv()
    w_sib.append(send(WF.at[y2, c, 0:hr], WF.at[y2, c, 0:hr], sib))
    w_far_down.wait_recv()
    w_sib.append(send(WF.at[y2, c, hr:rows], WF.at[y2, c, hr:rows], sib))

    for copy in cots:
        copy.wait_recv()
    br, bc = iota((512, 512), 0), iota((512, 512), 1)
    back = onehot(bc == (br & 15) * 32 + (br >> 4))
    cot_rows[...] = dot(back, cot_recv[...].reshape(512, 1024)).astype(bf16)

    for copy in w_sib:
        copy.wait_recv()
    for copy in arrive:
        copy.wait_recv()

    px, core, far, near, written = {}, {}, {}, {}, []
    cols = lambda j: slice(starts[j], starts[j] + sizes[j])

    def forward(j):
        part = None
        for kk in range(4):
            a = N[:, :, :, :, kk * chunk:(kk + 1) * chunk].reshape(512, chunk)
            b = WF[kk, :, :, cols(j)].reshape(chunk, sizes[j])
            p = dot(a, b)
            part = p if part is None else part + p
        part = part * scale
        R["acc%d" % j][...] = part
        out, got = R["px_send%d" % j], R["px_recv%d" % j]
        out[...] = part.astype(bf16)
        px[j] = send(out, got, x_pair)

    def pointwise(j):
        px[j].wait_recv()
        pre = R["acc%d" % j][...] + R["px_recv%d" % j][...].astype(f32)
        sig = jax.nn.sigmoid(pre)
        g = cot_rows[:, cols(j)].astype(f32) * sig * (1.0 + pre * (1.0 - sig))
        R["G%d" % j][...] = g.astype(bf16)

    def turned():
        for q in range(half // 256):
            part = N[:, :, :, :, q * 256:(q + 1) * 256].reshape(512, 256)
            NT[q * 256:(q + 1) * 256] = dot(eye, part, 1, 1).astype(bf16)

    order = (2, 1, 3, 0)

    def backward(j):
        g = R["G%d" % j][...]
        CS, CR = R["CS%d" % j], R["CR%d" % j]
        for d in order:
            base = m4(y + d) * chunk
            other = NT[pl.ds(pl.multiple_of(base + (1 - c) * rows, 16), rows)]
            CS[d] = (dot(other, g) * scale).astype(bf16)
            core[j, d] = send(CS.at[d], CR.at[d], sib)
            own = NT[pl.ds(pl.multiple_of(base + c * rows, 16), rows)]
            PB[d, :, :sizes[j]] = dot(own, g) * scale

    def join(j):
        S2, SL, SR, R2, RL, RR = (R["%s%d" % (n, j)] for n in ("S2", "SL", "SR", "R2", "RL", "RR"))
        for d in order:
            core[j, d].wait_recv()
            t = PB[d, :, :sizes[j]] + R["CR%d" % j][d].astype(f32)
            if d == 2:
                S2[...] = t.astype(bf16)
                far[j] = (send(S2.at[0:hr], R2.at[0], up), send(S2.at[hr:rows], R2.at[1], down))
            elif d == 1:
                SL[hr:rows] = t[hr:rows].astype(bf16)
                near[j] = [send(SL.at[hr:rows], RL.at[hr:rows], up)]
                R["keep%d" % j][0] = t[0:hr]
            elif d == 3:
                SR[0:hr] = t[0:hr].astype(bf16)
                near[j].append(send(SR.at[0:hr], RR.at[0:hr], down))
                R["keep%d" % j][1] = t[hr:rows]
            else:
                R["own%d" % j][...] = t

    def pass_on(j):
        SL, SR, R2, RL, RR = (R["%s%d" % (n, j)] for n in ("SL", "SR", "R2", "RL", "RR"))
        far[j][0].wait_recv()
        SL[0:hr] = (R["keep%d" % j][0] + R2[0].astype(f32)).astype(bf16)
        near[j].append(send(SL.at[0:hr], RL.at[0:hr], up))
        far[j][1].wait_recv()
        SR[hr:rows] = (R["keep%d" % j][1] + R2[1].astype(f32)).astype(bf16)
        near[j].append(send(SR.at[hr:rows], RR.at[hr:rows], down))

    def finish(j):
        for copy in near[j]:
            copy.wait_recv()
        grads = R["own%d" % j][...] + R["RL%d" % j][...].astype(f32) + R["RR%d" % j][...].astype(f32)
        stepped = WF[y, c, :, cols(j)].astype(f32) - inner_rate * grads
        for p in range(0, sizes[j], 128):
            f, at = (starts[j] + p) // 256, (starts[j] + p) % 256
            share = due[f][:, :128] * (1.0 - mix_share)
            new = stepped[:, p:p + 128] * (1.0 - share) + share * full_anchor[:, at:at + 128]
            R["out%d" % j][:, p:p + 128] = new.astype(bf16)
        copy = pltpu.make_async_copy(R["out%d" % j], out_hbm.at[:, cols(j)], lsem.at[3 + j])
        copy.start()
        written.append(copy)

    def outer_update():
        for copy in frags:
            copy.wait_recv()
        mean = f_recv[0].astype(f32)
        for i in range(1, 8):
            mean += f_recv[i].astype(f32)
        mean = mean[:, :rows] / 8
        anchor = anchor_ref[...]
        delta = anchor - mean
        new_mom = outer_decay * mom_ref[...] + delta
        new_anchor = anchor - outer_rate * (delta + outer_decay * new_mom)
        new_mom_ref[...] = new_mom
        new_anchor_ref[...] = new_anchor
        for i, (src, dst) in enumerate(((new_anchor_ref, new_anchor_hbm), (new_mom_ref, new_mom_hbm))):
            copy = pltpu.make_async_copy(src, dst, lsem.at[at_small + 4 + i])
            copy.start()
            written.append(copy)
        a_send[:, rows:] = jnp.zeros((32, a_send.shape[1] - rows), bf16)
        a_send[:, :rows] = new_anchor.astype(bf16)
        anchors = [send(a_send, a_recv.at[w], (worker_of(d, e), s)) for d, e in workers]
        a_recv[w] = a_send[...]
        return anchors

    def outer_spread():
        for copy in anchors:
            copy.wait_recv()
        full_anchor[...] = dot(a_recv[...].reshape(256, 512), eye, 0, 0)[:rows]

    for j in range(n_cols):
        forward(j)
    frags = [send(f_send.at[worker_of(d, e)], f_recv.at[w], (worker_of(d, e), s)) for d, e in workers]
    turned()
    pointwise(0)
    backward(0)
    join(0)
    for j in range(1, n_cols):
        pointwise(j)
        backward(j)
        join(j)
        pass_on(j - 1)
        if j == n_cols - 2:
            anchors = outer_update()
    outer_spread()
    for j in range(n_cols - 3):
        finish(j)
    pass_on(n_cols - 1)
    for j in range(n_cols - 3, n_cols):
        finish(j)
    for copy in written:
        copy.wait()
    done()


def shards(token_ids, cotangent, embedding, weight, anchor, momentum, due_fragment):
    rows, width = weight.shape[1], embedding.shape[1]
    half = width // 2
    anyspace = pl.BlockSpec(memory_space=pl.ANY)
    V, DMA = pltpu.VMEM, pltpu.SemaphoreType.DMA
    sizes = (128, 128, 256, 256, 128, 128)
    n_sends = 200
    scratch = {
        "emb": V((128, width), bf16),
        "normed": V((128, width), bf16),
        "cot": V((256, 1024), bf16),
        "ids_g": V((8, 8, 256), i32),
        "ids_all": V((16, 8, 256), i32),
        "SS": V((2, 4, 4, 16, half), bf16),
        "RA": V((4, 4, 16, half), bf16),
        "RB": V((4, 4, 16, half), bf16),
        "N": V((4, 4, 2, 16, half), bf16),
        "NT": V((half, 512), bf16),
        "WF": V((4, 2, rows, 1024), bf16),
        "cot_send": V((8, 32, 1024), bf16),
        "cot_far": V((8, 32, 1024), bf16),
        "cot_recv": V((16, 32, 1024), bf16),
        "cot_rows": V((512, 1024), bf16),
        "fpad": V((512, 256), bf16),
        "f_send": V((8, 32, 512), bf16),
        "f_recv": V((8, 32, 512), bf16),
        "a_send": V((32, 512), bf16),
        "a_recv": V((8, 32, 512), bf16),
        "full_anchor": V((rows, 256), f32),
        "PB": V((4, rows, 256), f32),
        "ids": V((1, 256), i32),
        "due": pltpu.SMEM((1,), i32),
        "anchor": V(anchor.shape[::-1], f32),
        "mom": V(anchor.shape[::-1], f32),
        "new_anchor": V(anchor.shape[::-1], f32),
        "new_mom": V(anchor.shape[::-1], f32),
        "lsem": DMA((9 + len(sizes),)),
        "ssem": DMA((n_sends,)),
        "rsem": DMA((n_sends,)),
    }
    for j, n in enumerate(sizes):
        scratch["acc%d" % j] = V((512, n), f32)
        scratch["px_send%d" % j] = V((512, n), bf16)
        scratch["px_recv%d" % j] = V((512, n), bf16)
        scratch["G%d" % j] = V((512, n), bf16)
        scratch["keep%d" % j] = V((2, rows // 2, n), f32)
        scratch["CS%d" % j] = V((4, rows, n), bf16)
        scratch["CR%d" % j] = V((4, rows, n), bf16)
        scratch["R2%d" % j] = V((2, rows // 2, n), bf16)
        scratch["own%d" % j] = V((rows, n), f32)
        for name in ("S2", "SL", "SR", "RL", "RR", "out"):
            scratch["%s%d" % (name, j)] = V((rows, n), bf16)
    new_weight, new_anchor, new_momentum = pl.pallas_call(
        functools.partial(kernel, tuple(scratch), sizes),
        out_shape=(
            jax.ShapeDtypeStruct((rows, 1024), bf16),
            jax.ShapeDtypeStruct(anchor.shape[::-1], f32),
            jax.ShapeDtypeStruct(anchor.shape[::-1], f32),
        ),
        in_specs=[anyspace] * 7,
        out_specs=(anyspace,) * 3,
        scratch_shapes=list(scratch.values()),
        compiler_params=pltpu.CompilerParams(
            collective_id=0, has_side_effects=True, vmem_limit_bytes=60 * 2**20
        ),
        cost_estimate=pl.CostEstimate(flops=7_500_000_000, bytes_accessed=5_000_000, transcendentals=262144),
        name="diloco_step",
    )(token_ids.reshape(1, 256), due_fragment, anchor.T, momentum.T, embedding, weight.reshape(rows, 1024), cotangent)
    return (new_weight[None], new_anchor.T, new_momentum.T)


def solution(mesh):
    placed = (
        P(("worker", "shard")),
        P(("worker", "shard"), None),
        P(("worker", "shard"), None),
        P("worker", "shard", None),
        P("shard", "worker"),
        P("shard", "worker"),
        P(),
    )
    return jax.shard_map(
        shards,
        mesh=mesh,
        in_specs=placed,
        out_specs=(P("worker", "shard", None), P("shard", "worker"), P("shard", "worker")),
        check_vma=False,
    )
```
